512 devices in a mesh: row: 16 (over x_hi, y), col: 32 (over z, x_lo, core).
Axes of the slice: x: 4 (x_hi: 2, x_lo: 2; x = x_hi * 2 + x_lo), y: 8, z: 8, core: 2. Of those that a mesh axis runs over, the one named last changes fastest.
Arguments:
- tiles: bfloat16 [1024, 1024, 1024], P(('row', 'col')), may hold values from 0 to 12288, as said below
- tile_blocks: int32 [1024, 2], P(('row', 'col')), may hold values from 0 to 63, as said below
- tile_count: int32 [512], P(('row', 'col')), may hold values from 1 to 2, as said below
- factor: float32 [2, 2, 16, 32, 32, 128], P(None, None, 'row', 'col'), may hold values from 0.2 to 5
Outputs:
- factor_out: float32 [2, 2, 16, 32, 32, 128], P(None, None, 'row', 'col')
The draws below stay inside these ranges and needn't reach their ends.
Inputs may be any that keep to these rules, and one draw needn't show every extreme that they name: `tile_blocks`: slot s belongs to the device of index s // 2 along row+col, with grid indices (r, c); its (i, j) has i <= j, i % 16 == r and j % 32 == c. A device's live slots are its first tile_count entries. `tiles`: tiles are nonnegative.
All inputs are finite; a program needn't handle non-finite values.
Results may differ from the reference program's by a relative error of at most 0.0003.
Values may be sent and summed in bfloat16 or wider, within the bound.
A program may use at most 64 MiB of HBM per device.

```python
import math
import jax
import jax.numpy as jnp
from jax import lax

K = 128
BS = 1024
PC = 2
TILES_DEV = 2
ITERS = 2
MULT = 2
NB = 64
SLICE = 32
TILES = 1024
N_ROW = 16
N_COL = 32


def draw_tile_blocks(key, part):
    key = jax.random.fold_in(key, 11)
    column_count = NB // PC
    row_count = column_count // MULT
    slot_ids = jnp.arange(TILES, dtype=jnp.int32)
    device = slot_ids // TILES_DEV
    grid_row = device // column_count
    grid_column = device % column_count
    key_column, key_row = jax.random.split(key)
    lowest = (grid_column < grid_row).astype(jnp.int32)
    column_step = jax.random.randint(key_column, (TILES,), lowest, PC)
    column_step = jnp.where(slot_ids == TILES - TILES_DEV, PC - 1, column_step)
    column_index = grid_column + column_count * column_step
    highest = (column_index - grid_row) // row_count
    row_step = jax.random.randint(key_row, (TILES,), 0, highest + 1)
    row_step = jnp.where(slot_ids == 0, 0, row_step)
    row_index = grid_row + row_count * row_step
    return jnp.stack([row_index, column_index], axis=1).astype(jnp.int32)


def draw_tile_count(key, part):
    key = jax.random.fold_in(key, 12)
    counts = jax.random.randint(key, (TILES // TILES_DEV,), 1, TILES_DEV + 1)
    counts = counts.at[0].set(TILES_DEV)
    return counts.astype(jnp.int32)


def draw_tiles(key, part):
    key = jax.random.fold_in(key, 13)
    key_mask, key_value = jax.random.split(key, 2)
    magnitude = 12.0 * MULT * PC * PC * K
    present = jax.random.bernoulli(key_mask, 0.5, (TILES, BS, BS)).astype(jnp.float32)
    base = jax.random.uniform(key_value, (TILES, BS, BS), jnp.float32, 0.0, 1.0)
    values = base ** 16
    return (present * values * magnitude).astype(jnp.bfloat16)


def block_levels(key, shape, cuts, least, high):
    gain = 1.0
    for dim, blocks in cuts:
        steps = jax.random.uniform(jax.random.fold_in(jax.random.fold_in(key, 6), dim), (blocks,), jnp.float32, least / len(cuts), high / len(cuts))
        gain = gain * jnp.repeat(jnp.exp(steps), shape[dim] // blocks).reshape((-1,) + (1,) * (len(shape) - 1 - dim))
    return gain


def setup_inputs(seed: int = 0) -> dict:
    key_of = jax.random.split(jax.random.key(seed), 5)
    tiles = draw_tiles(jax.random.fold_in(key_of[4], 71), 0)
    tile_blocks = draw_tile_blocks(jax.random.fold_in(key_of[4], 71), 0)
    tile_count = draw_tile_count(jax.random.fold_in(key_of[4], 71), 0)
    factor = jnp.clip(jnp.exp(math.log(5.0) - 3.218876 * jax.random.uniform(key_of[3], (PC, MULT, N_ROW, N_COL, SLICE, K), jnp.float32) ** block_levels(key_of[3], (PC, MULT, N_ROW, N_COL, SLICE, K), ((2, 16), (3, 32)), -0.2, 0.2)), 0.2, 5.0)
    return dict(tiles=tiles, tile_blocks=tile_blocks, tile_count=tile_count, factor=factor)


def reference(tiles, tile_blocks, tile_count, factor):
    factor_now = factor.reshape(NB, BS, K)
    slot_ids = jnp.arange(TILES, dtype=jnp.int32)
    live_mask = (slot_ids % TILES_DEV < tile_count[slot_ids // TILES_DEV]).astype(jnp.float32)
    row_blocks = tile_blocks[:, 0].astype(jnp.int32)
    column_blocks = tile_blocks[:, 1].astype(jnp.int32)
    off_diagonal = (row_blocks != column_blocks).astype(jnp.float32) * live_mask
    for sweep in range(ITERS):
        rounded = factor_now.astype(jnp.bfloat16)
        flattened = rounded.reshape(NB * BS, K)
        gram_matrix = lax.dot_general(flattened, flattened, (((0,), (0,)), ((), ())), preferred_element_type=jnp.float32)
        rounded_float = rounded.astype(jnp.float32)

        def add_tile(accumulated, scan_item):
            block_tile, row_index, column_index, row_weight, column_weight = scan_item
            tile_float = block_tile.astype(jnp.float32)
            right_rows = lax.dynamic_index_in_dim(rounded_float, column_index, 0, keepdims=False)
            left_rows = lax.dynamic_index_in_dim(rounded_float, row_index, 0, keepdims=False)
            row_term = jnp.dot(tile_float, right_rows, precision=lax.Precision.HIGHEST) * row_weight
            column_term = jnp.dot(tile_float.T, left_rows, precision=lax.Precision.HIGHEST) * column_weight
            accumulated = accumulated.at[row_index].add(row_term)
            accumulated = accumulated.at[column_index].add(column_term)
            return accumulated, None

        start_sum = jnp.zeros((NB, BS, K), jnp.float32)
        product, _ = lax.scan(add_tile, start_sum, (tiles, row_blocks, column_blocks, live_mask, off_diagonal))
        denominator = jnp.dot(factor_now.reshape(NB * BS, K), gram_matrix, precision=lax.Precision.HIGHEST).reshape(NB, BS, K)
        factor_now = factor_now * (0.5 + 0.5 * product / denominator)
    return factor_now.reshape(factor.shape)
```

```python
import jax
import jax.numpy as jnp
from jax import lax
from jax.experimental import pallas as pl
from jax.experimental.pallas import tpu as pltpu
from jax.sharding import PartitionSpec as P

ITERS = 2
MESH = pl.DeviceIdType.MESH
F32 = jnp.float32
BF16 = jnp.bfloat16
N_KEYS = 112
LAST = (4, 3)


def kernel(
    blocks, count, tiles_hbm, f_ref, o_ref,
    tiles, rp, cp, rs, cr, zb, cs, yb, xs, xr, fr, gm, gr, gf, terms,
    tile_sem, send_sem, recv_sem, gram_send, gram_recv,
):
    r = lax.axis_index("row")
    c = lax.axis_index("col")
    xh, y = r // 8, r % 8
    z, q = c // 4, c % 4
    xi, ka = q // 2, q % 2

    def spread(t):
        return (t % 8 + (1 + 3 * (t // 4) + 2 * (t % 4)) % 4) % 8

    holder_y = (z + 2 * q + spread(r)) % 8
    holders = [[(h * 8 + holder_y, r + 16 * k) for h in range(2)] for k in range(2)]
    owner_row = c % 16
    column_k = c // 16
    shift = spread(owner_row)
    owner_z = [(y + 16 - 2 * w - shift) % 8 for w in range(4)]
    owners = [(owner_row, owner_z[w] * 4 + w) for w in range(4)]

    core_peer = (r, z * 4 + xi * 2 + (1 - ka))
    x_peer = (r, z * 4 + (1 - xi) * 2 + ka)
    z_next = [(r, ((z + 1) % 8) * 4 + q), (r, ((z + 7) % 8) * 4 + q)]
    y_next = [(xh * 8 + (y + 1) % 8, c), (xh * 8 + (y + 7) % 8, c)]

    tile_copy = pltpu.make_async_copy(tiles_hbm, tiles, tile_sem)
    tile_copy.start()

    barrier = pltpu.get_barrier_semaphore()
    near = [core_peer, x_peer] + z_next + holders[0] + holders[1] + owners
    for device in near:
        pl.semaphore_signal(barrier, inc=1, device_id=device, device_id_type=MESH)

    def greet(d, carry):
        pl.semaphore_signal(barrier, inc=1, device_id=((r + d) % 16, c), device_id_type=MESH)
        return carry

    lax.fori_loop(1, 16, greet, 0)
    o_ref[...] = f_ref[...]
    pl.semaphore_wait(barrier, len(near) + 15)

    def chunk_of(pos, direction, slot):
        return (pos + 3 - slot) % 8 if direction == 0 else (pos + 6 + slot) % 8

    def sweep(it, carry):
        keys = {}
        sends = []

        def number(key):
            return keys.setdefault(key, len(keys))

        def push(key, src, dst, device):
            n = number(key)
            copy = pltpu.make_async_remote_copy(
                src_ref=src, dst_ref=dst, send_sem=send_sem.at[n], recv_sem=recv_sem.at[it, n],
                device_id=device, device_id_type=MESH,
            )
            copy.start()
            sends.append(copy)

        def arrived(key, dst):
            n = number(key)
            pltpu.make_async_remote_copy(
                src_ref=dst, dst_ref=dst, send_sem=send_sem.at[n], recv_sem=recv_sem.at[it, n],
                device_id=core_peer, device_id_type=MESH,
            ).wait_recv()

        rp[it, z, xi, ka] = o_ref[...].astype(BF16)
        mine = rp.at[it, z, xi, ka]
        for k in range(2):
            for h in range(2):
                n = number(("scatter", k, h))
                copy = pltpu.make_async_remote_copy(
                    src_ref=rp.at[it, z, xi, ka, :, k], dst_ref=cp.at[it, holder_y, q],
                    send_sem=send_sem.at[n], recv_sem=recv_sem.at[it, N_KEYS - 4 + q],
                    device_id=holders[k][h], device_id_type=MESH,
                )
                copy.start()
                sends.append(copy)

        def chain(h):
            return xi if h == 0 else 1 - xi

        def row_piece(pos, h):
            return rp.at[it, pos, chain(h), ka]

        def column_piece(pos, h):
            return cp.at[it, pos, 2 * h:2 * h + 2]

        def pass_row(direction, step, h):
            pos = (z + 8 - step) % 8 if direction == 0 else (z + step) % 8
            piece = row_piece(pos, h)
            if step > 0:
                arrived(("zg", direction, step, h), piece)
            if step < LAST[direction]:
                push(("zg", direction, step + 1, h), piece, piece, z_next[direction])
            if step > 0 or direction == 0:
                push(("cg", direction, step, h), piece, piece, core_peer)

        def pass_column(direction, step, h):
            pos = (y + 8 - step) % 8 if direction == 0 else (y + step) % 8
            piece = column_piece(pos, h)
            if step > 0:
                arrived(("yg", direction, step, h), piece)
            if step < LAST[direction]:
                push(("yg", direction, step + 1, h), piece, piece, y_next[direction])

        push(("x",), mine, mine, x_peer)
        for direction in range(2):
            pass_row(direction, 0, 0)
        arrived(("x",), row_piece(z, 1))
        for direction in range(2):
            pass_row(direction, 0, 1)
        for h in range(2):
            for w in (2 * h, 2 * h + 1):
                pltpu.make_async_remote_copy(
                    src_ref=cp.at[it, y, w], dst_ref=cp.at[it, y, w],
                    send_sem=send_sem.at[0], recv_sem=recv_sem.at[it, N_KEYS - 4 + w],
                    device_id=core_peer, device_id_type=MESH,
                ).wait_recv()
            for direction in range(2):
                pass_column(direction, 0, h)
        for step in range(1, 5):
            for h in range(2):
                for direction in range(2):
                    if step <= LAST[direction]:
                        pass_row(direction, step, h)
                        pass_column(direction, step, h)
        for step in range(0, 5):
            for h in range(2):
                for direction in range(2):
                    if step <= LAST[direction] and (step > 0 or direction == 0):
                        pos = (z + 8 - step) % 8 if direction == 0 else (z + step) % 8
                        arrived(("cg", direction, step, h), rp.at[it, pos, chain(h), 1 - ka])

        @pl.when(it == 0)
        def _():
            tile_copy.wait()

        live = [(count[0] > s).astype(F32) for s in range(2)]
        off = [(blocks[s, 0] != blocks[s, 1]).astype(F32) for s in range(2)]
        row_slot = [blocks[s, 0] // 16 for s in range(2)]
        column_slot = [blocks[s, 1] // 32 for s in range(2)]

        for s in range(2):
            left = rp[it, :, :, :, row_slot[s] // 2, row_slot[s] % 2].reshape(1024, 128).T
            for n in range(4):
                term = jnp.dot(left, tiles[s, :, n * 256:(n + 1) * 256], preferred_element_type=F32)
                terms[s, n * 256:(n + 1) * 256, :] = term.T
        for p in range(2):
            weight = [live[s] * off[s] * (column_slot[s] == p).astype(F32) for s in range(2)]
            for v in range(32):
                rows = slice(v * 32, v * 32 + 32)
                cs[it, (v // 4 + 2 * (v % 4) + shift) % 8, v % 4, p] = (
                    weight[0] * terms[0, rows] + weight[1] * terms[1, rows]
                )

        def column_sum(pos, h):
            return cs.at[it, pos, 2 * h:2 * h + 2]

        for h in range(2):
            for direction, far in ((0, 4), (1, 5)):
                push(
                    ("yr", direction, 0, h), column_sum((y + far) % 8, h),
                    yb.at[it, direction, 0, h], y_next[direction],
                )

        for s in range(2):
            right = jnp.concatenate(
                [
                    cp[it, (v // 4 + 2 * (v % 4) + shift) % 8, v % 4, column_slot[s]]
                    for v in range(32)
                ],
                axis=0,
            )
            for n in range(4):
                rows = slice(n * 256, (n + 1) * 256)
                terms[s, rows, :] = jnp.dot(tiles[s, rows, :], right, preferred_element_type=F32)
        for slot in range(4):
            weight = [live[s] * (row_slot[s] == slot).astype(F32) for s in range(2)]
            both = weight[0] * terms[0] + weight[1] * terms[1]
            rs[it, :, :, :, slot // 2, slot % 2] = both.reshape(8, 2, 2, 32, 128)

        order = (4, 5, 3, 6, 2, 7, 1, 0)
        for far in order:
            pos = (z + far) % 8
            push(("cr", far), rs.at[it, pos, :, 1 - ka], cr.at[it, pos], core_peer)

        total = jnp.zeros((128, 128), F32)
        for slot in range(4):
            panel = rp[it, :, :, :, slot // 2, slot % 2].reshape(1024, 128)
            total = total + jnp.dot(panel.T, panel, preferred_element_type=F32)
        gm[it] = total.reshape(16, 8, 128)

        def gram_scatter(d, carry):
            pltpu.make_async_remote_copy(
                src_ref=gm.at[it, (r + d) % 16], dst_ref=gr.at[it, d - 1],
                send_sem=gram_send.at[0], recv_sem=gram_recv.at[it, 0],
                device_id=((r + d) % 16, c), device_id_type=MESH,
            ).start()
            return carry

        def gram_gather(d, carry):
            pltpu.make_async_remote_copy(
                src_ref=gf.at[it, r], dst_ref=gf.at[it, r],
                send_sem=gram_send.at[1], recv_sem=gram_recv.at[it, 1],
                device_id=((r + d) % 16, c), device_id_type=MESH,
            ).start()
            return carry

        def bytes_of_fifteen(sem):
            pltpu.make_async_copy(gr.at[it], gr.at[it], sem).wait()

        lax.fori_loop(1, 16, gram_scatter, 0)

        def own_row(pos, h):
            return rs[it, pos, h, ka] + cr[it, pos, h]

        def pass_row_sum(direction, slot, h):
            pos = chunk_of(z, direction, slot)
            buf = zb.at[it, direction, slot, h]
            arrived(("zr", direction, slot, h), buf)
            if h == 0:
                arrived(("cr", (3 - slot) if direction == 0 else (6 + slot)), cr.at[it, pos])
            zb[it, direction, slot, h] += own_row(pos, h)
            push(("zr", direction, slot + 1, h), buf, zb.at[it, direction, slot + 1, h], z_next[direction])

        def pass_column_sum(direction, slot, h):
            pos = chunk_of(y, direction, slot)
            buf = yb.at[it, direction, slot, h]
            arrived(("yr", direction, slot, h), buf)
            yb[it, direction, slot, h] += cs[it, pos, 2 * h:2 * h + 2]
            push(("yr", direction, slot + 1, h), buf, yb.at[it, direction, slot + 1, h], y_next[direction])

        for direction, far in ((0, 4), (1, 5)):
            pos = (z + far) % 8
            arrived(("cr", far), cr.at[it, pos])
            for h in range(2):
                rs[it, pos, h, ka] = own_row(pos, h)
                push(
                    ("zr", direction, 0, h), rs.at[it, pos, h, ka],
                    zb.at[it, direction, 0, h], z_next[direction],
                )
        for slot in range(3):
            for h in range(2):
                for direction in range(2):
                    if slot < LAST[direction] - 1:
                        pass_column_sum(direction, slot, h)
                        pass_row_sum(direction, slot, h)
            if slot == 0:
                bytes_of_fifteen(gram_recv.at[it, 0])
                gf[it, r] = gm[it, r] + jnp.sum(gr[it], axis=0)
                lax.fori_loop(1, 16, gram_gather, 0)

        for h in range(2):
            for direction in range(2):
                slot = LAST[direction] - 1
                arrived(("yr", direction, slot, h), yb.at[it, direction, slot, h])
            yb[it, 0, 3, h] += cs[it, y, 2 * h:2 * h + 2] + yb[it, 1, 2, h]
            for w in range(2):
                n = number(("owner", 2 * h + w))
                copy = pltpu.make_async_remote_copy(
                    src_ref=yb.at[it, 0, 3, h, w], dst_ref=fr.at[it, column_k, xh],
                    send_sem=send_sem.at[n], recv_sem=recv_sem.at[it, N_KEYS - 8 + column_k * 2 + xh],
                    device_id=owners[2 * h + w], device_id_type=MESH,
                )
                copy.start()
                sends.append(copy)
        arrived(("cr", 0), cr.at[it, z])
        for h in range(2):
            for direction in range(2):
                slot = LAST[direction] - 1
                arrived(("zr", direction, slot, h), zb.at[it, direction, slot, h])
            xs[it, h] = own_row(z, h) + zb[it, 0, 3, h] + zb[it, 1, 2, h]
        push(("xr",), xs.at[it, 1 - xi], xr.at[it], x_peer)

        bytes_of_fifteen(gram_recv.at[it, 1])
        held = o_ref[...]
        below = jnp.dot(
            held.reshape(128, 128), gf[it].reshape(128, 128),
            precision=lax.Precision.HIGHEST, preferred_element_type=F32,
        ).reshape(2, 2, 32, 128)
        arrived(("xr",), xr.at[it])
        for k in range(2):
            for h in range(2):
                pltpu.make_async_remote_copy(
                    src_ref=fr.at[it, k, h], dst_ref=fr.at[it, k, h],
                    send_sem=send_sem.at[0], recv_sem=recv_sem.at[it, N_KEYS - 8 + k * 2 + h],
                    device_id=core_peer, device_id_type=MESH,
                ).wait_recv()
        product = xs[it, xi] + xr[it]
        for k in range(2):
            above = product[:, k] + (fr[it, k, 0] + fr[it, k, 1])
            o_ref[:, k] = held[:, k] * (0.5 + 0.5 * above / below[:, k])

        for copy in sends:
            copy.wait_send()
        for phase in range(2):
            bytes_of_fifteen(gram_send.at[phase])
        assert len(keys) <= N_KEYS - 8
        return carry

    lax.fori_loop(0, ITERS, sweep, 0)


def shards(tiles, tile_blocks, tile_count, factor):
    vmem = pl.BlockSpec(memory_space=pltpu.VMEM)
    smem = pl.BlockSpec(memory_space=pltpu.SMEM)
    held = pl.pallas_call(
        kernel,
        out_shape=jax.ShapeDtypeStruct((2, 2, 32, 128), F32),
        in_specs=[smem, smem, pl.BlockSpec(memory_space=pl.ANY), vmem],
        out_specs=vmem,
        scratch_shapes=[
            pltpu.VMEM((2, 1024, 1024), BF16),
            pltpu.VMEM((2, 8, 2, 2, 2, 2, 32, 128), BF16),
            pltpu.VMEM((2, 8, 4, 2, 32, 128), BF16),
            pltpu.VMEM((2, 8, 2, 2, 2, 2, 32, 128), F32),
            pltpu.VMEM((2, 8, 2, 2, 2, 32, 128), F32),
            pltpu.VMEM((2, 2, 4, 2, 2, 2, 32, 128), F32),
            pltpu.VMEM((2, 8, 4, 2, 32, 128), F32),
            pltpu.VMEM((2, 2, 4, 2, 2, 2, 32, 128), F32),
            pltpu.VMEM((2, 2, 2, 2, 32, 128), F32),
            pltpu.VMEM((2, 2, 2, 32, 128), F32),
            pltpu.VMEM((2, 2, 2, 2, 32, 128), F32),
            pltpu.VMEM((2, 16, 8, 128), F32),
            pltpu.VMEM((2, 15, 8, 128), F32),
            pltpu.VMEM((2, 16, 8, 128), F32),
            pltpu.VMEM((2, 1024, 128), F32),
            pltpu.SemaphoreType.DMA,
            pltpu.SemaphoreType.DMA((N_KEYS,)),
            pltpu.SemaphoreType.DMA((2, N_KEYS)),
            pltpu.SemaphoreType.DMA((2,)),
            pltpu.SemaphoreType.DMA((2, 2)),
        ],
        compiler_params=pltpu.CompilerParams(
            collective_id=0, has_side_effects=True, vmem_limit_bytes=50 * 1024 * 1024
        ),
    )(tile_blocks, tile_count, tiles, factor.reshape(2, 2, 32, 128))
    return held.reshape(factor.shape)


def solution(mesh):
    in_specs = (
        P(("row", "col"), None, None),
        P(("row", "col"), None),
        P(("row", "col")),
        P(None, None, "row", "col", None, None),
    )
    out_specs = P(None, None, "row", "col", None, None)
    return jax.shard_map(shards, mesh=mesh, in_specs=in_specs, out_specs=out_specs, check_vma=False)
```

```python
import jax
import jax.numpy as jnp
from jax import lax
from jax.experimental import pallas as pl
from jax.experimental.pallas import tpu as pltpu
from jax.sharding import PartitionSpec as P

ITERS = 2
MESH = pl.DeviceIdType.MESH
F32 = jnp.float32
BF16 = jnp.bfloat16
N_KEYS = 112


def hops(direction, h):
    return 4 if direction == h else 3


def kernel(
    blocks, count, tiles_hbm, f_ref, o_ref,
    tiles, rp, cp, rs, cr, zb, cs, yb, xs, xr, fr, gm, gr, gf, terms, right, yo, fa, fm,
    tile_sem, send_sem, recv_sem, gram_send, gram_recv,
):
    r = lax.axis_index("row")
    c = lax.axis_index("col")
    xh, y = r // 8, r % 8
    z, q = c // 4, c % 4
    xi, ka = q // 2, q % 2

    def spread(t):
        b3, b2, b1, b0 = t // 8, (t // 4) % 2, (t // 2) % 2, t % 2
        return ((2 * b1 + 2 * b3 + 1 - b2 + b0 + 2 * b2 * b0) % 4 + 4 * b2) % 8

    holder_y = (z + 2 * q + spread(r)) % 8
    holders = [[(h * 8 + holder_y, r + 16 * k) for h in range(2)] for k in range(2)]
    owner_row = c % 16
    column_k = c // 16
    shift = spread(owner_row)
    owner_z = [(y + 16 - 2 * w - shift) % 8 for w in range(4)]
    owners = [(owner_row, owner_z[w] * 4 + w) for w in range(4)]

    stations = [
        ((owner_row // 8) * 8 + y, owner_z[w] * 4 + (1 - xi) * 2 + 1 - w % 2) for w in range(4)
    ]
    my_station = (xh * 8 + holder_y, z * 4 + (1 - (r // 2) % 2) * 2 + 1 - ka)
    base = (y + 24 - z - 2 * (1 - ka) - 2 * (1 - xi) - 2 * xh) % 4
    served_row = 8 * xh + 4 * (1 - ((base + 1) % 4) // 2) + 2 * (1 - xi) + base // 2
    served = (served_row, z * 4 + ((y + 16 - z - spread(served_row)) % 8) // 2)
    feeders = [(h * 8 + y, served_row + 16 * k) for k in range(2) for h in range(2)]

    core_peer = (r, z * 4 + xi * 2 + (1 - ka))
    x_peer = (r, z * 4 + (1 - xi) * 2 + ka)
    z_next = [(r, ((z + 1) % 8) * 4 + q), (r, ((z + 7) % 8) * 4 + q)]
    y_next = [(xh * 8 + (y + 1) % 8, c), (xh * 8 + (y + 7) % 8, c)]

    tile_copy = pltpu.make_async_copy(tiles_hbm, tiles, tile_sem)
    tile_copy.start()

    barrier = pltpu.get_barrier_semaphore()
    near = [core_peer, x_peer] + z_next + owners + feeders + [my_station]
    for device in near:
        pl.semaphore_signal(barrier, inc=1, device_id=device, device_id_type=MESH)

    def greet(d, carry):
        pl.semaphore_signal(barrier, inc=1, device_id=((r + d) % 16, c), device_id_type=MESH)
        return carry

    lax.fori_loop(1, 16, greet, 0)
    o_ref[...] = f_ref[...]
    pl.semaphore_wait(barrier, len(near) + 15)

    def source_of(pos, direction, step):
        return (pos + 8 - step) % 8 if direction == 0 else (pos + step) % 8

    def sweep(it, carry):
        keys = {}
        sends = []

        def number(key):
            return keys.setdefault(key, len(keys))

        def push(key, src, dst, device):
            n = number(key)
            copy = pltpu.make_async_remote_copy(
                src_ref=src, dst_ref=dst, send_sem=send_sem.at[n], recv_sem=recv_sem.at[it, n],
                device_id=device, device_id_type=MESH,
            )
            copy.start()
            sends.append(copy)

        def arrived(key, dst):
            n = number(key)
            pltpu.make_async_remote_copy(
                src_ref=dst, dst_ref=dst, send_sem=send_sem.at[n], recv_sem=recv_sem.at[it, n],
                device_id=core_peer, device_id_type=MESH,
            ).wait_recv()

        rp[it, z, xi, ka] = o_ref[...].astype(BF16)
        mine = rp.at[it, z, xi, ka]
        for k in range(2):
            for h in range(2):
                n = number(("scatter", k, h))
                copy = pltpu.make_async_remote_copy(
                    src_ref=rp.at[it, z, xi, ka, :, k], dst_ref=cp.at[it, holder_y, q],
                    send_sem=send_sem.at[n], recv_sem=recv_sem.at[it, N_KEYS - 4 + q],
                    device_id=holders[k][h], device_id_type=MESH,
                )
                copy.start()
                sends.append(copy)

        def chain(h):
            return xi if h == 0 else 1 - xi

        def row_piece(pos, h):
            return rp.at[it, pos, chain(h), ka]

        def column_piece(pos, h):
            return cp.at[it, pos, 2 * h:2 * h + 2]

        def pass_row(direction, step, h):
            pos = source_of(z, direction, step)
            piece = row_piece(pos, h)
            if step > 0:
                arrived(("zg", direction, step, h), piece)
            if step < hops(direction, h):
                push(("zg", direction, step + 1, h), piece, piece, z_next[direction])

        def pass_column(direction, step, h):
            piece = column_piece(source_of(y, direction, step), h)
            if step > 0:
                arrived(("yg", direction, step, h), piece)
            if step < hops(direction, h):
                push(("yg", direction, step + 1, h), piece, piece, y_next[direction])

        def directions(step):
            return (0, 1) if 0 < step < 4 else (0,)

        def across(step):
            for direction in directions(step):
                pieces = rp.at[it, source_of(z, direction, step), :, ka]
                push(("cg", direction, step), pieces, pieces, core_peer)

        def each(passing, step):
            for h in range(2):
                for direction in range(2):
                    if step <= hops(direction, h):
                        passing(direction, step, h)

        live = [(count[0] > s).astype(F32) for s in range(2)]
        off = [(blocks[s, 0] != blocks[s, 1]).astype(F32) for s in range(2)]
        row_slot = [blocks[s, 0] // 16 for s in range(2)]
        is_row = [[(row_slot[s] == slot).astype(F32) for slot in range(4)] for s in range(2)]
        column_slot = [blocks[s, 1] // 32 for s in range(2)]

        def tile_rows(s, pos, columns):
            return tiles[s, pl.ds(pl.multiple_of(pos * 128, 128), 128), columns]

        def joined(parts):
            return parts[0] if len(parts) == 1 else jnp.concatenate(parts, axis=0)

        def chosen(s, pos):
            total = None
            for slot in range(4):
                part = is_row[s][slot] * rp[it, pos, :, :, slot // 2, slot % 2].astype(F32)
                total = part if total is None else total + part
            return total.reshape(128, 128).astype(BF16)

        def panel_step(step):
            for direction in directions(step):
                arrived(("cg", direction, step), rp.at[it, source_of(z, direction, step), :, 1 - ka])
            places = [source_of(z, direction, step) for direction in directions(step)]
            for s in range(2):
                left = joined([chosen(s, pos) for pos in places]).T
                for n in range(4):
                    columns = slice(n * 256, (n + 1) * 256)
                    term = jnp.dot(
                        left, joined([tile_rows(s, pos, columns) for pos in places]),
                        preferred_element_type=F32,
                    )
                    if step == 0:
                        terms[s, :, columns] = term
                    else:
                        terms[s, :, columns] += term
            total = None
            for pos in places:
                panel = rp[it, pos].reshape(512, 128)
                part = jnp.dot(panel.T, panel, preferred_element_type=F32).reshape(16, 8, 128)
                total = part if total is None else total + part
            if step == 0:
                gm[it] = total
            else:
                gm[it] += total

        push(("x",), mine, mine, x_peer)
        for direction in range(2):
            pass_row(direction, 0, 0)
        arrived(("x",), row_piece(z, 1))
        for direction in range(2):
            pass_row(direction, 0, 1)
        across(0)
        each(pass_row, 1)
        across(1)
        for h in range(2):
            for w in (2 * h, 2 * h + 1):
                pltpu.make_async_remote_copy(
                    src_ref=cp.at[it, y, w], dst_ref=cp.at[it, y, w],
                    send_sem=send_sem.at[0], recv_sem=recv_sem.at[it, N_KEYS - 4 + w],
                    device_id=core_peer, device_id_type=MESH,
                ).wait_recv()
            for direction in range(2):
                pass_column(direction, 0, h)
        each(pass_row, 2)
        across(2)
        each(pass_column, 1)

        @pl.when(it == 0)
        def _():
            tile_copy.wait()

        panel_step(0)
        each(pass_row, 3)
        across(3)
        each(pass_column, 2)
        panel_step(1)
        each(pass_row, 4)
        across(4)
        each(pass_column, 3)
        panel_step(2)
        panel_step(3)
        panel_step(4)
        for p in range(2):
            weight = [live[s] * off[s] * (column_slot[s] == p).astype(F32) for s in range(2)]
            for n in range(8):
                columns = slice(n * 128, (n + 1) * 128)
                both = (weight[0] * terms[0, :, columns] + weight[1] * terms[1, :, columns]).T
                for w in range(4):
                    cs[it, (n + 2 * w + shift) % 8, w, p] = both[w * 32:w * 32 + 32]

        def distance(direction, h, slot):
            ahead = hops(direction, h) - 1 - slot
            return ahead if direction == 0 else (8 - ahead) % 8

        chains = ((0, 0), (1, 1), (0, 1), (1, 0))
        for direction, h in chains:
            push(
                ("yr", direction, 0, h), cs.at[it, (y + distance(direction, h, -1)) % 8, 2 * h:2 * h + 2],
                yb.at[it, direction, 0, h], y_next[direction],
            )
        each(pass_column, 4)

        for s in range(2):
            for v in range(32):
                right[s, v * 32:v * 32 + 32, :] = cp[
                    it, (v // 4 + 2 * (v % 4) + shift) % 8, v % 4, column_slot[s]
                ]

        def row_chunks(fars):
            places = [(z + far) % 8 for far in fars]
            term = [
                jnp.dot(
                    joined([tile_rows(s, pos, slice(None)) for pos in places]), right[s],
                    preferred_element_type=F32,
                )
                for s in range(2)
            ]
            for slot in range(4):
                weight = [live[s] * (row_slot[s] == slot).astype(F32) for s in range(2)]
                both = weight[0] * term[0] + weight[1] * term[1]
                for n, pos in enumerate(places):
                    for w in range(4):
                        rows = slice(n * 128 + w * 32, n * 128 + w * 32 + 32)
                        rs[it, pos, w % 2, w // 2, slot // 2, slot % 2] = both[rows]
            for far, pos in zip(fars, places):
                push(("cr", far), rs.at[it, pos, 1 - ka], cr.at[it, pos], core_peer)

        row_chunks((4,))
        row_chunks((3, 5))
        met = set()

        def own_row(far, h):
            pos = (z + far) % 8
            if far not in met:
                met.add(far)
                arrived(("cr", far), cr.at[it, pos])
            return rs[it, pos, ka, h] + cr[it, pos, h]

        def own_column(far, h):
            return cs[it, (y + far) % 8, 2 * h:2 * h + 2]

        def first_sums(direction, h):
            far = distance(direction, h, -1)
            pos = (z + far) % 8
            rs[it, pos, ka, h] = own_row(far, h)
            push(
                ("zr", direction, 0, h), rs.at[it, pos, ka, h],
                zb.at[it, direction, 0, h], z_next[direction],
            )

        def pass_sums(slot):
            for direction, h in chains:
                if slot < hops(direction, h) - 1:
                    far = distance(direction, h, slot)
                    buf = yb.at[it, direction, slot, h]
                    arrived(("yr", direction, slot, h), buf)
                    yb[it, direction, slot, h] += own_column(far, h)
                    push(("yr", direction, slot + 1, h), buf, yb.at[it, direction, slot + 1, h], y_next[direction])
                    buf = zb.at[it, direction, slot, h]
                    arrived(("zr", direction, slot, h), buf)
                    zb[it, direction, slot, h] += own_row(far, h)
                    push(("zr", direction, slot + 1, h), buf, zb.at[it, direction, slot + 1, h], z_next[direction])

        for direction, h in chains:
            first_sums(direction, h)

        def gram_scatter(d, carry):
            pltpu.make_async_remote_copy(
                src_ref=gm.at[it, (r + d) % 16], dst_ref=gr.at[it, d - 1],
                send_sem=gram_send.at[0], recv_sem=gram_recv.at[it, 0],
                device_id=((r + d) % 16, c), device_id_type=MESH,
            ).start()
            return carry

        def gram_gather(d, carry):
            pltpu.make_async_remote_copy(
                src_ref=gf.at[it, r], dst_ref=gf.at[it, r],
                send_sem=gram_send.at[1], recv_sem=gram_recv.at[it, 1],
                device_id=((r + d) % 16, c), device_id_type=MESH,
            ).start()
            return carry

        def bytes_of_fifteen(sem):
            pltpu.make_async_copy(gr.at[it], gr.at[it], sem).wait()

        lax.fori_loop(1, 16, gram_scatter, 0)
        row_chunks((2, 6))
        pass_sums(0)
        row_chunks((1, 7))
        pass_sums(1)
        row_chunks((0,))
        bytes_of_fifteen(gram_recv.at[it, 0])
        gf[it, r] = gm[it, r] + jnp.sum(gr[it], axis=0)
        lax.fori_loop(1, 16, gram_gather, 0)
        pass_sums(2)

        def last_sums(box, name, h):
            total = None
            for direction in range(2):
                slot = hops(direction, h) - 1
                arrived((name, direction, slot, h), box.at[it, direction, slot, h])
                part = box[it, direction, slot, h]
                total = part if total is None else total + part
            return total

        for h in range(2):
            yo[it, h] = own_column(0, h) + last_sums(yb, "yr", h)
            for w in range(2):
                n = number(("owner", 2 * h + w))
                copy = pltpu.make_async_remote_copy(
                    src_ref=yo.at[it, h, w], dst_ref=fa.at[it, xh, column_k],
                    send_sem=send_sem.at[n], recv_sem=recv_sem.at[it, N_KEYS - 8 + column_k * 2 + xh],
                    device_id=stations[2 * h + w], device_id_type=MESH,
                )
                copy.start()
                sends.append(copy)
        for k in range(2):
            for h in range(2):
                pltpu.make_async_remote_copy(
                    src_ref=fa.at[it, h, k], dst_ref=fa.at[it, h, k],
                    send_sem=send_sem.at[0], recv_sem=recv_sem.at[it, N_KEYS - 8 + k * 2 + h],
                    device_id=core_peer, device_id_type=MESH,
                ).wait_recv()
        fm[it] = fa[it, 0] + fa[it, 1]
        push(("home",), fm.at[it], fr.at[it], served)
        for h in range(2):
            xs[it, h] = own_row(0, h) + last_sums(zb, "zr", h)
        push(("xr",), xs.at[it, 1 - xi], xr.at[it], x_peer)

        bytes_of_fifteen(gram_recv.at[it, 1])
        held = o_ref[...]
        below = jnp.dot(
            held.reshape(128, 128), gf[it].reshape(128, 128),
            precision=lax.Precision.HIGHEST, preferred_element_type=F32,
        ).reshape(2, 2, 32, 128)
        arrived(("xr",), xr.at[it])
        arrived(("home",), fr.at[it])
        product = xs[it, xi] + xr[it]
        for k in range(2):
            above = product[:, k] + fr[it, k]
            o_ref[:, k] = held[:, k] * (0.5 + 0.5 * above / below[:, k])

        for copy in sends:
            copy.wait_send()
        for phase in range(2):
            bytes_of_fifteen(gram_send.at[phase])
        assert len(keys) <= N_KEYS - 8
        return carry

    lax.fori_loop(0, ITERS, sweep, 0)


def shards(tiles, tile_blocks, tile_count, factor):
    vmem = pl.BlockSpec(memory_space=pltpu.VMEM)
    smem = pl.BlockSpec(memory_space=pltpu.SMEM)
    held = pl.pallas_call(
        kernel,
        out_shape=jax.ShapeDtypeStruct((2, 2, 32, 128), F32),
        in_specs=[smem, smem, pl.BlockSpec(memory_space=pl.ANY), vmem],
        out_specs=vmem,
        scratch_shapes=[
            pltpu.VMEM((2, 1024, 1024), BF16),
            pltpu.VMEM((2, 8, 2, 2, 2, 2, 32, 128), BF16),
            pltpu.VMEM((2, 8, 4, 2, 32, 128), BF16),
            pltpu.VMEM((2, 8, 2, 2, 2, 2, 32, 128), F32),
            pltpu.VMEM((2, 8, 2, 2, 2, 32, 128), F32),
            pltpu.VMEM((2, 2, 4, 2, 2, 2, 32, 128), F32),
            pltpu.VMEM((2, 8, 4, 2, 32, 128), F32),
            pltpu.VMEM((2, 2, 4, 2, 2, 2, 32, 128), F32),
            pltpu.VMEM((2, 2, 2, 2, 32, 128), F32),
            pltpu.VMEM((2, 2, 2, 32, 128), F32),
            pltpu.VMEM((2, 2, 2, 32, 128), F32),
            pltpu.VMEM((2, 16, 8, 128), F32),
            pltpu.VMEM((2, 15, 8, 128), F32),
            pltpu.VMEM((2, 16, 8, 128), F32),
            pltpu.VMEM((2, 128, 1024), F32),
            pltpu.VMEM((2, 1024, 128), BF16),
            pltpu.VMEM((2, 2, 2, 2, 32, 128), F32),
            pltpu.VMEM((2, 2, 2, 2, 32, 128), F32),
            pltpu.VMEM((2, 2, 2, 32, 128), F32),
            pltpu.SemaphoreType.DMA,
            pltpu.SemaphoreType.DMA((N_KEYS,)),
            pltpu.SemaphoreType.DMA((2, N_KEYS)),
            pltpu.SemaphoreType.DMA((2,)),
            pltpu.SemaphoreType.DMA((2, 2)),
        ],
        compiler_params=pltpu.CompilerParams(
            collective_id=0, has_side_effects=True, vmem_limit_bytes=50 * 1024 * 1024
        ),
    )(tile_blocks, tile_count, tiles, factor.reshape(2, 2, 32, 128))
    return held.reshape(factor.shape)


def solution(mesh):
    in_specs = (
        P(("row", "col"), None, None),
        P(("row", "col"), None),
        P(("row", "col")),
        P(None, None, "row", "col", None, None),
    )
    out_specs = P(None, None, "row", "col", None, None)
    return jax.shard_map(shards, mesh=mesh, in_specs=in_specs, out_specs=out_specs, check_vma=False)
```

```python
import jax
import jax.numpy as jnp
from jax import lax
from jax.experimental import pallas as pl
from jax.experimental.pallas import tpu as pltpu
from jax.sharding import PartitionSpec as P

ITERS = 2
MESH = pl.DeviceIdType.MESH
F32 = jnp.float32
BF16 = jnp.bfloat16
N_KEYS = 112


def hops(direction, h):
    return 4 if direction == h else 3


def kernel(
    blocks, count, tiles_hbm, f_ref, o_ref,
    tiles, rp, cp, rs, cr, zb, cs, yb, xs, xr, fr, gm, gr, gf, terms, right, yo, fa, fm,
    tile_sem, send_sem, recv_sem, gram_send, gram_recv,
):
    r = lax.axis_index("row")
    c = lax.axis_index("col")
    xh, y = r // 8, r % 8
    z, q = c // 4, c % 4
    xi, ka = q // 2, q % 2

    def spread(t):
        b3, b2, b1, b0 = t // 8, (t // 4) % 2, (t // 2) % 2, t % 2
        return ((2 * b1 + 2 * b3 + 1 - b2 + b0 + 2 * b2 * b0) % 4 + 4 * b2) % 8

    holder_y = (z + 2 * q + spread(r)) % 8
    holders = [[(h * 8 + holder_y, r + 16 * k) for h in range(2)] for k in range(2)]
    owner_row = c % 16
    column_k = c // 16
    shift = spread(owner_row)
    owner_z = [(y + 16 - 2 * w - shift) % 8 for w in range(4)]
    owners = [(owner_row, owner_z[w] * 4 + w) for w in range(4)]

    stations = [
        ((owner_row // 8) * 8 + y, owner_z[w] * 4 + (1 - xi) * 2 + 1 - w % 2) for w in range(4)
    ]
    my_station = (xh * 8 + holder_y, z * 4 + (1 - (r // 2) % 2) * 2 + 1 - ka)
    base = (y + 24 - z - 2 * (1 - ka) - 2 * (1 - xi) - 2 * xh) % 4
    served_row = 8 * xh + 4 * (1 - ((base + 1) % 4) // 2) + 2 * (1 - xi) + base // 2
    served = (served_row, z * 4 + ((y + 16 - z - spread(served_row)) % 8) // 2)
    feeders = [(h * 8 + y, served_row + 16 * k) for k in range(2) for h in range(2)]

    core_peer = (r, z * 4 + xi * 2 + (1 - ka))
    x_peer = (r, z * 4 + (1 - xi) * 2 + ka)
    z_next = [(r, ((z + 1) % 8) * 4 + q), (r, ((z + 7) % 8) * 4 + q)]
    y_next = [(xh * 8 + (y + 1) % 8, c), (xh * 8 + (y + 7) % 8, c)]

    tile_copy = pltpu.make_async_copy(tiles_hbm, tiles, tile_sem)
    tile_copy.start()

    barrier = pltpu.get_barrier_semaphore()
    near = [core_peer, x_peer] + z_next + owners + feeders + [my_station]
    for device in near:
        pl.semaphore_signal(barrier, inc=1, device_id=device, device_id_type=MESH)

    def greet(d, carry):
        pl.semaphore_signal(barrier, inc=1, device_id=((r + d) % 16, c), device_id_type=MESH)
        return carry

    lax.fori_loop(1, 16, greet, 0)
    o_ref[...] = f_ref[...]
    pl.semaphore_wait(barrier, len(near) + 15)

    def source_of(pos, direction, step):
        return (pos + 8 - step) % 8 if direction == 0 else (pos + step) % 8

    def sweep(it, carry):
        keys = {}
        sends = []

        def number(key):
            return keys.setdefault(key, len(keys))

        def push(key, src, dst, device):
            n = number(key)
            copy = pltpu.make_async_remote_copy(
                src_ref=src, dst_ref=dst, send_sem=send_sem.at[n], recv_sem=recv_sem.at[it, n],
                device_id=device, device_id_type=MESH,
            )
            copy.start()
            sends.append(copy)

        def arrived(key, dst):
            n = number(key)
            pltpu.make_async_remote_copy(
                src_ref=dst, dst_ref=dst, send_sem=send_sem.at[n], recv_sem=recv_sem.at[it, n],
                device_id=core_peer, device_id_type=MESH,
            ).wait_recv()

        rp[it, z, xi, ka] = o_ref[...].astype(BF16)
        mine = rp.at[it, z, xi, ka]
        for k in range(2):
            for h in range(2):
                n = number(("scatter", k, h))
                copy = pltpu.make_async_remote_copy(
                    src_ref=rp.at[it, z, xi, ka, :, k], dst_ref=cp.at[it, holder_y, q],
                    send_sem=send_sem.at[n], recv_sem=recv_sem.at[it, N_KEYS - 4 + q],
                    device_id=holders[k][h], device_id_type=MESH,
                )
                copy.start()
                sends.append(copy)

        def chain(h):
            return xi if h == 0 else 1 - xi

        def row_piece(pos, h):
            return rp.at[it, pos, chain(h), ka]

        def column_piece(pos, h):
            return cp.at[it, pos, 2 * h:2 * h + 2]

        def pass_row(direction, step, h):
            pos = source_of(z, direction, step)
            piece = row_piece(pos, h)
            if step > 0:
                arrived(("zg", direction, step, h), piece)
            if step < hops(direction, h):
                push(("zg", direction, step + 1, h), piece, piece, z_next[direction])

        def pass_column(direction, step, h):
            piece = column_piece(source_of(y, direction, step), h)
            if step > 0:
                arrived(("yg", direction, step, h), piece)
            if step < hops(direction, h):
                push(("yg", direction, step + 1, h), piece, piece, y_next[direction])

        def directions(step):
            return (0, 1) if 0 < step < 4 else (0,)

        def across(step):
            for direction in directions(step):
                pieces = rp.at[it, source_of(z, direction, step), :, ka]
                push(("cg", direction, step), pieces, pieces, core_peer)

        def each(passing, step):
            for h in range(2):
                for direction in range(2):
                    if step <= hops(direction, h):
                        passing(direction, step, h)

        live = [(count[0] > s).astype(F32) for s in range(2)]
        off = [(blocks[s, 0] != blocks[s, 1]).astype(F32) for s in range(2)]
        row_slot = [blocks[s, 0] // 16 for s in range(2)]
        is_row = [[(row_slot[s] == slot).astype(F32) for slot in range(4)] for s in range(2)]
        column_slot = [blocks[s, 1] // 32 for s in range(2)]

        def tile_rows(s, pos, columns):
            return tiles[s, pl.ds(pl.multiple_of(pos * 128, 128), 128), columns]

        def joined(parts):
            return parts[0] if len(parts) == 1 else jnp.concatenate(parts, axis=0)

        def chosen(s, pos):
            total = None
            for slot in range(4):
                part = is_row[s][slot] * rp[it, pos, :, :, slot // 2, slot % 2].astype(F32)
                total = part if total is None else total + part
            return total.reshape(128, 128).astype(BF16)

        def panel_step(step):
            for direction in directions(step):
                arrived(("cg", direction, step), rp.at[it, source_of(z, direction, step), :, 1 - ka])
            places = [source_of(z, direction, step) for direction in directions(step)]
            for s in range(2):
                left = joined([chosen(s, pos) for pos in places]).T
                for n in range(4):
                    columns = slice(n * 256, (n + 1) * 256)
                    term = jnp.dot(
                        left, joined([tile_rows(s, pos, columns) for pos in places]),
                        preferred_element_type=F32,
                    )
                    if step == 0:
                        terms[s, :, columns] = term
                    else:
                        terms[s, :, columns] += term
            total = None
            for pos in places:
                panel = rp[it, pos].reshape(512, 128)
                part = jnp.dot(panel.T, panel, preferred_element_type=F32).reshape(16, 8, 128)
                total = part if total is None else total + part
            if step == 0:
                gm[it] = total
            else:
                gm[it] += total

        push(("x",), mine, mine, x_peer)
        for direction in range(2):
            pass_row(direction, 0, 0)
        arrived(("x",), row_piece(z, 1))
        for direction in range(2):
            pass_row(direction, 0, 1)
        across(0)
        each(pass_row, 1)
        across(1)
        for h in range(2):
            for w in (2 * h, 2 * h + 1):
                pltpu.make_async_remote_copy(
                    src_ref=cp.at[it, y, w], dst_ref=cp.at[it, y, w],
                    send_sem=send_sem.at[0], recv_sem=recv_sem.at[it, N_KEYS - 4 + w],
                    device_id=core_peer, device_id_type=MESH,
                ).wait_recv()
            for direction in range(2):
                pass_column(direction, 0, h)
        each(pass_row, 2)
        across(2)
        each(pass_column, 1)

        @pl.when(it == 0)
        def _():
            tile_copy.wait()

        panel_step(0)
        each(pass_row, 3)
        across(3)
        each(pass_column, 2)
        panel_step(1)
        each(pass_row, 4)
        across(4)
        each(pass_column, 3)
        panel_step(2)
        panel_step(3)
        panel_step(4)
        for p in range(2):
            weight = [live[s] * off[s] * (column_slot[s] == p).astype(F32) for s in range(2)]
            for n in range(8):
                columns = slice(n * 128, (n + 1) * 128)
                both = (weight[0] * terms[0, :, columns] + weight[1] * terms[1, :, columns]).T
                for w in range(4):
                    cs[it, (n + 2 * w + shift) % 8, w, p] = both[w * 32:w * 32 + 32]

        def distance(direction, h, slot):
            ahead = hops(direction, h) - 1 - slot
            return ahead if direction == 0 else (8 - ahead) % 8

        chains = ((0, 0), (1, 1), (0, 1), (1, 0))
        for direction, h in chains:
            push(
                ("yr", direction, 0, h), cs.at[it, (y + distance(direction, h, -1)) % 8, 2 * h:2 * h + 2],
                yb.at[it, direction, 0, h], y_next[direction],
            )
        each(pass_column, 4)

        for s in range(2):
            for v in range(32):
                right[s, v * 32:v * 32 + 32, :] = cp[
                    it, (v // 4 + 2 * (v % 4) + shift) % 8, v % 4, column_slot[s]
                ]

        def row_chunks(fars):
            places = [(z + far) % 8 for far in fars]
            term = [
                jnp.dot(
                    joined([tile_rows(s, pos, slice(None)) for pos in places]), right[s],
                    preferred_element_type=F32,
                )
                for s in range(2)
            ]
            for slot in range(4):
                weight = [live[s] * (row_slot[s] == slot).astype(F32) for s in range(2)]
                both = weight[0] * term[0] + weight[1] * term[1]
                for n, pos in enumerate(places):
                    for w in range(4):
                        rows = slice(n * 128 + w * 32, n * 128 + w * 32 + 32)
                        rs[it, pos, w % 2, w // 2, slot // 2, slot % 2] = both[rows]
            for far, pos in zip(fars, places):
                push(("cr", far), rs.at[it, pos, 1 - ka], cr.at[it, pos], core_peer)

        met = set()

        def own_row(far, h):
            pos = (z + far) % 8
            if far not in met:
                met.add(far)
                arrived(("cr", far), cr.at[it, pos])
            return rs[it, pos, ka, h] + cr[it, pos, h]

        def own_column(far, h):
            return cs[it, (y + far) % 8, 2 * h:2 * h + 2]

        def first_sums(direction, h):
            far = distance(direction, h, -1)
            pos = (z + far) % 8
            rs[it, pos, ka, h] = own_row(far, h)
            push(
                ("zr", direction, 0, h), rs.at[it, pos, ka, h],
                zb.at[it, direction, 0, h], z_next[direction],
            )

        def column_sums(slot):
            for direction, h in chains:
                if slot < hops(direction, h) - 1:
                    buf = yb.at[it, direction, slot, h]
                    arrived(("yr", direction, slot, h), buf)
                    yb[it, direction, slot, h] += own_column(distance(direction, h, slot), h)
                    push(("yr", direction, slot + 1, h), buf, yb.at[it, direction, slot + 1, h], y_next[direction])

        def row_sums(slot):
            for direction, h in chains:
                if slot < hops(direction, h) - 1:
                    buf = zb.at[it, direction, slot, h]
                    arrived(("zr", direction, slot, h), buf)
                    zb[it, direction, slot, h] += own_row(distance(direction, h, slot), h)
                    push(("zr", direction, slot + 1, h), buf, zb.at[it, direction, slot + 1, h], z_next[direction])

        def gram_scatter(d, carry):
            pltpu.make_async_remote_copy(
                src_ref=gm.at[it, (r + d) % 16], dst_ref=gr.at[it, d - 1],
                send_sem=gram_send.at[0], recv_sem=gram_recv.at[it, 0],
                device_id=((r + d) % 16, c), device_id_type=MESH,
            ).start()
            return carry

        def gram_gather(d, carry):
            pltpu.make_async_remote_copy(
                src_ref=gf.at[it, r], dst_ref=gf.at[it, r],
                send_sem=gram_send.at[1], recv_sem=gram_recv.at[it, 1],
                device_id=((r + d) % 16, c), device_id_type=MESH,
            ).start()
            return carry

        def bytes_of_fifteen(sem):
            pltpu.make_async_copy(gr.at[it], gr.at[it], sem).wait()

        def last_sums(box, name, h):
            total = None
            for direction in range(2):
                slot = hops(direction, h) - 1
                arrived((name, direction, slot, h), box.at[it, direction, slot, h])
                part = box[it, direction, slot, h]
                total = part if total is None else total + part
            return total

        row_chunks((4,))
        row_chunks((3, 5))
        column_sums(0)
        for direction, h in chains:
            first_sums(direction, h)
        lax.fori_loop(1, 16, gram_scatter, 0)
        row_chunks((2, 6))
        column_sums(1)
        row_sums(0)
        row_chunks((1, 7))
        column_sums(2)
        row_sums(1)
        row_chunks((0,))
        bytes_of_fifteen(gram_recv.at[it, 0])
        gf[it, r] = gm[it, r] + jnp.sum(gr[it], axis=0)
        lax.fori_loop(1, 16, gram_gather, 0)
        for h in range(2):
            yo[it, h] = own_column(0, h) + last_sums(yb, "yr", h)
            for w in range(2):
                n = number(("owner", 2 * h + w))
                copy = pltpu.make_async_remote_copy(
                    src_ref=yo.at[it, h, w], dst_ref=fa.at[it, xh, column_k],
                    send_sem=send_sem.at[n], recv_sem=recv_sem.at[it, N_KEYS - 8 + column_k * 2 + xh],
                    device_id=stations[2 * h + w], device_id_type=MESH,
                )
                copy.start()
                sends.append(copy)
        row_sums(2)
        for h in range(2):
            xs[it, h] = own_row(0, h) + last_sums(zb, "zr", h)
        push(("xr",), xs.at[it, 1 - xi], xr.at[it], x_peer)
        for k in range(2):
            for h in range(2):
                pltpu.make_async_remote_copy(
                    src_ref=fa.at[it, h, k], dst_ref=fa.at[it, h, k],
                    send_sem=send_sem.at[0], recv_sem=recv_sem.at[it, N_KEYS - 8 + k * 2 + h],
                    device_id=core_peer, device_id_type=MESH,
                ).wait_recv()
        fm[it] = fa[it, 0] + fa[it, 1]
        push(("home",), fm.at[it], fr.at[it], served)

        bytes_of_fifteen(gram_recv.at[it, 1])
        held = o_ref[...]
        below = jnp.dot(
            held.reshape(128, 128), gf[it].reshape(128, 128),
            precision=lax.Precision.HIGHEST, preferred_element_type=F32,
        ).reshape(2, 2, 32, 128)
        arrived(("xr",), xr.at[it])
        arrived(("home",), fr.at[it])
        product = xs[it, xi] + xr[it]
        for k in range(2):
            above = product[:, k] + fr[it, k]
            o_ref[:, k] = held[:, k] * (0.5 + 0.5 * above / below[:, k])

        for copy in sends:
            copy.wait_send()
        for phase in range(2):
            bytes_of_fifteen(gram_send.at[phase])
        assert len(keys) <= N_KEYS - 8
        return carry

    lax.fori_loop(0, ITERS, sweep, 0)


def shards(tiles, tile_blocks, tile_count, factor):
    vmem = pl.BlockSpec(memory_space=pltpu.VMEM)
    smem = pl.BlockSpec(memory_space=pltpu.SMEM)
    held = pl.pallas_call(
        kernel,
        out_shape=jax.ShapeDtypeStruct((2, 2, 32, 128), F32),
        in_specs=[smem, smem, pl.BlockSpec(memory_space=pl.ANY), vmem],
        out_specs=vmem,
        scratch_shapes=[
            pltpu.VMEM((2, 1024, 1024), BF16),
            pltpu.VMEM((2, 8, 2, 2, 2, 2, 32, 128), BF16),
            pltpu.VMEM((2, 8, 4, 2, 32, 128), BF16),
            pltpu.VMEM((2, 8, 2, 2, 2, 2, 32, 128), F32),
            pltpu.VMEM((2, 8, 2, 2, 2, 32, 128), F32),
            pltpu.VMEM((2, 2, 4, 2, 2, 2, 32, 128), F32),
            pltpu.VMEM((2, 8, 4, 2, 32, 128), F32),
            pltpu.VMEM((2, 2, 4, 2, 2, 2, 32, 128), F32),
            pltpu.VMEM((2, 2, 2, 2, 32, 128), F32),
            pltpu.VMEM((2, 2, 2, 32, 128), F32),
            pltpu.VMEM((2, 2, 2, 32, 128), F32),
            pltpu.VMEM((2, 16, 8, 128), F32),
            pltpu.VMEM((2, 15, 8, 128), F32),
            pltpu.VMEM((2, 16, 8, 128), F32),
            pltpu.VMEM((2, 128, 1024), F32),
            pltpu.VMEM((2, 1024, 128), BF16),
            pltpu.VMEM((2, 2, 2, 2, 32, 128), F32),
            pltpu.VMEM((2, 2, 2, 2, 32, 128), F32),
            pltpu.VMEM((2, 2, 2, 32, 128), F32),
            pltpu.SemaphoreType.DMA,
            pltpu.SemaphoreType.DMA((N_KEYS,)),
            pltpu.SemaphoreType.DMA((2, N_KEYS)),
            pltpu.SemaphoreType.DMA((2,)),
            pltpu.SemaphoreType.DMA((2, 2)),
        ],
        compiler_params=pltpu.CompilerParams(
            collective_id=0, has_side_effects=True, vmem_limit_bytes=50 * 1024 * 1024
        ),
    )(tile_blocks, tile_count, tiles, factor.reshape(2, 2, 32, 128))
    return held.reshape(factor.shape)


def solution(mesh):
    in_specs = (
        P(("row", "col"), None, None),
        P(("row", "col"), None),
        P(("row", "col")),
        P(None, None, "row", "col", None, None),
    )
    out_specs = P(None, None, "row", "col", None, None)
    return jax.shard_map(shards, mesh=mesh, in_specs=in_specs, out_specs=out_specs, check_vma=False)
```

```python
import jax
import jax.numpy as jnp
from jax import lax
from jax.experimental import pallas as pl
from jax.experimental.pallas import tpu as pltpu
from jax.sharding import PartitionSpec as P

ITERS = 2
MESH = pl.DeviceIdType.MESH
F32 = jnp.float32
BF16 = jnp.bfloat16
N_KEYS = 144


def hops(direction, h):
    return 4 if direction == h else 3


def kernel(
    blocks, count, tiles_hbm, f_ref, o_ref,
    tiles, rp, cp, rs, cr, zb, cs, yb, xs, xr, fr, gm, gr, gf, terms, right, yo, fa, fm,
    tile_sem, send_sem, recv_sem, gram_send, gram_recv,
):
    r = lax.axis_index("row")
    c = lax.axis_index("col")
    xh, y = r // 8, r % 8
    z, q = c // 4, c % 4
    xi, ka = q // 2, q % 2

    def spread(t):
        b3, b2, b1, b0 = t // 8, (t // 4) % 2, (t // 2) % 2, t % 2
        return ((2 * b1 + 2 * b3 + 1 - b2 + b0 + 2 * b2 * b0) % 4 + 4 * b2) % 8

    holder_y = (z + 2 * q + spread(r)) % 8
    holders = [[(h * 8 + holder_y, r + 16 * k) for h in range(2)] for k in range(2)]
    owner_row = c % 16
    column_k = c // 16
    shift = spread(owner_row)
    owner_z = [(y + 16 - 2 * w - shift) % 8 for w in range(4)]
    owners = [(owner_row, owner_z[w] * 4 + w) for w in range(4)]

    stations = [
        ((owner_row // 8) * 8 + y, owner_z[w] * 4 + (1 - xi) * 2 + 1 - w % 2) for w in range(4)
    ]
    my_station = (xh * 8 + holder_y, z * 4 + (1 - (r // 2) % 2) * 2 + 1 - ka)
    base = (y + 24 - z - 2 * (1 - ka) - 2 * (1 - xi) - 2 * xh) % 4
    served_row = 8 * xh + 4 * (1 - ((base + 1) % 4) // 2) + 2 * (1 - xi) + base // 2
    served = (served_row, z * 4 + ((y + 16 - z - spread(served_row)) % 8) // 2)
    feeders = [(h * 8 + y, served_row + 16 * k) for k in range(2) for h in range(2)]

    core_peer = (r, z * 4 + xi * 2 + (1 - ka))
    x_peer = (r, z * 4 + (1 - xi) * 2 + ka)
    z_next = [(r, ((z + 1) % 8) * 4 + q), (r, ((z + 7) % 8) * 4 + q)]
    y_next = [(xh * 8 + (y + 1) % 8, c), (xh * 8 + (y + 7) % 8, c)]

    tile_copy = pltpu.make_async_copy(tiles_hbm, tiles, tile_sem)
    tile_copy.start()

    barrier = pltpu.get_barrier_semaphore()
    near = [core_peer, x_peer] + z_next + owners + feeders + [my_station]
    for device in near:
        pl.semaphore_signal(barrier, inc=1, device_id=device, device_id_type=MESH)

    def greet(d, carry):
        pl.semaphore_signal(barrier, inc=1, device_id=((r + d) % 16, c), device_id_type=MESH)
        return carry

    lax.fori_loop(1, 16, greet, 0)
    o_ref[...] = f_ref[...]
    pl.semaphore_wait(barrier, len(near) + 15)

    def source_of(pos, direction, step):
        return (pos + 8 - step) % 8 if direction == 0 else (pos + step) % 8

    def sweep(it, carry):
        keys = {}
        sends = []

        def number(key):
            return keys.setdefault(key, len(keys))

        def push(key, src, dst, device):
            n = number(key)
            copy = pltpu.make_async_remote_copy(
                src_ref=src, dst_ref=dst, send_sem=send_sem.at[n], recv_sem=recv_sem.at[it, n],
                device_id=device, device_id_type=MESH,
            )
            copy.start()
            sends.append(copy)

        def arrived(key, dst):
            n = number(key)
            pltpu.make_async_remote_copy(
                src_ref=dst, dst_ref=dst, send_sem=send_sem.at[n], recv_sem=recv_sem.at[it, n],
                device_id=core_peer, device_id_type=MESH,
            ).wait_recv()

        rp[it, z, xi, ka] = o_ref[...].astype(BF16)
        mine = rp.at[it, z, xi, ka]
        for k in range(2):
            for h in range(2):
                n = number(("scatter", k, h))
                copy = pltpu.make_async_remote_copy(
                    src_ref=rp.at[it, z, xi, ka, :, k], dst_ref=cp.at[it, holder_y, q],
                    send_sem=send_sem.at[n], recv_sem=recv_sem.at[it, N_KEYS - 4 + q],
                    device_id=holders[k][h], device_id_type=MESH,
                )
                copy.start()
                sends.append(copy)

        def chain(h):
            return xi if h == 0 else 1 - xi

        def row_piece(pos, h):
            return rp.at[it, pos, chain(h), ka]

        def pass_row(direction, step, h):
            pos = source_of(z, direction, step)
            piece = row_piece(pos, h)
            if step > 0:
                arrived(("zg", direction, step, h), piece)
            if step < hops(direction, h):
                push(("zg", direction, step + 1, h), piece, piece, z_next[direction])

        def pass_column(direction, step, h):
            pos = source_of(y, direction, step)
            for w in (2 * h, 2 * h + 1):
                piece = cp.at[it, pos, w]
                if step > 0:
                    arrived(("yg", direction, step, w), piece)
                if step < hops(direction, h):
                    push(("yg", direction, step + 1, w), piece, piece, y_next[direction])

        def directions(step):
            return (0, 1) if 0 < step < 4 else (0,)

        def across(step):
            for direction in directions(step):
                pieces = rp.at[it, source_of(z, direction, step), :, ka]
                push(("cg", direction, step), pieces, pieces, core_peer)

        def each(passing, step):
            for h in range(2):
                for direction in range(2):
                    if step <= hops(direction, h):
                        passing(direction, step, h)

        live = [(count[0] > s).astype(F32) for s in range(2)]
        off = [(blocks[s, 0] != blocks[s, 1]).astype(F32) for s in range(2)]
        row_slot = [blocks[s, 0] // 16 for s in range(2)]
        is_row = [[(row_slot[s] == slot).astype(F32) for slot in range(4)] for s in range(2)]
        column_slot = [blocks[s, 1] // 32 for s in range(2)]

        def tile_rows(s, pos, columns):
            return tiles[s, pl.ds(pl.multiple_of(pos * 128, 128), 128), columns]

        def joined(parts):
            return parts[0] if len(parts) == 1 else jnp.concatenate(parts, axis=0)

        def chosen(s, pos):
            total = None
            for slot in range(4):
                part = is_row[s][slot] * rp[it, pos, :, :, slot // 2, slot % 2].astype(F32)
                total = part if total is None else total + part
            return total.reshape(128, 128).astype(BF16)

        def panel_step(step):
            for direction in directions(step):
                arrived(("cg", direction, step), rp.at[it, source_of(z, direction, step), :, 1 - ka])
            places = [source_of(z, direction, step) for direction in directions(step)]
            for s in range(2):
                left = joined([chosen(s, pos) for pos in places]).T
                for n in range(4):
                    columns = slice(n * 256, (n + 1) * 256)
                    term = jnp.dot(
                        left, joined([tile_rows(s, pos, columns) for pos in places]),
                        preferred_element_type=F32,
                    )
                    if step == 0:
                        terms[s, :, columns] = term
                    else:
                        terms[s, :, columns] += term

        push(("x",), mine, mine, x_peer)
        for direction in range(2):
            pass_row(direction, 0, 0)
        arrived(("x",), row_piece(z, 1))
        for direction in range(2):
            pass_row(direction, 0, 1)
        across(0)
        each(pass_row, 1)
        across(1)
        for h in range(2):
            for w in (2 * h, 2 * h + 1):
                pltpu.make_async_remote_copy(
                    src_ref=cp.at[it, y, w], dst_ref=cp.at[it, y, w],
                    send_sem=send_sem.at[0], recv_sem=recv_sem.at[it, N_KEYS - 4 + w],
                    device_id=core_peer, device_id_type=MESH,
                ).wait_recv()
            for direction in range(2):
                pass_column(direction, 0, h)
        each(pass_row, 2)
        across(2)
        each(pass_column, 1)

        @pl.when(it == 0)
        def _():
            tile_copy.wait()

        panel_step(0)
        each(pass_row, 3)
        across(3)
        each(pass_column, 2)
        panel_step(1)
        each(pass_row, 4)
        across(4)
        each(pass_column, 3)
        panel_step(2)
        panel_step(3)
        panel_step(4)
        for p in range(2):
            weight = [live[s] * off[s] * (column_slot[s] == p).astype(F32) for s in range(2)]
            for n in range(8):
                columns = slice(n * 128, (n + 1) * 128)
                both = (weight[0] * terms[0, :, columns] + weight[1] * terms[1, :, columns]).T
                for w in range(4):
                    cs[it, (n + 2 * w + shift) % 8, w, p] = both[w * 32:w * 32 + 32]

        def distance(direction, h, slot):
            ahead = hops(direction, h) - 1 - slot
            return ahead if direction == 0 else (8 - ahead) % 8

        chains = ((0, 0), (1, 1), (0, 1), (1, 0))
        for direction, h in chains:
            for w in (2 * h, 2 * h + 1):
                push(
                    ("yr", direction, 0, w), cs.at[it, (y + distance(direction, h, -1)) % 8, w],
                    yb.at[it, direction, 0, w], y_next[direction],
                )
        each(pass_column, 4)

        for s in range(2):
            for v in range(32):
                right[s, v * 32:v * 32 + 32, :] = cp[
                    it, (v // 4 + 2 * (v % 4) + shift) % 8, v % 4, column_slot[s]
                ]

        def row_chunks(fars):
            places = [(z + far) % 8 for far in fars]
            term = [
                jnp.dot(
                    joined([tile_rows(s, pos, slice(None)) for pos in places]), right[s],
                    preferred_element_type=F32,
                )
                for s in range(2)
            ]
            for slot in range(4):
                weight = [live[s] * (row_slot[s] == slot).astype(F32) for s in range(2)]
                both = weight[0] * term[0] + weight[1] * term[1]
                for n, pos in enumerate(places):
                    for w in range(4):
                        rows = slice(n * 128 + w * 32, n * 128 + w * 32 + 32)
                        rs[it, pos, w % 2, w // 2, slot // 2, slot % 2] = both[rows]
            for far, pos in zip(fars, places):
                push(("cr", far), rs.at[it, pos, 1 - ka], cr.at[it, pos], core_peer)

        met = set()

        def own_row(far, h, p):
            pos = (z + far) % 8
            if far not in met:
                met.add(far)
                arrived(("cr", far), cr.at[it, pos])
            return rs[it, pos, ka, h, p] + cr[it, pos, h, p]

        def own_column(far, w):
            return cs[it, (y + far) % 8, w]

        def first_sums(direction, h, p):
            far = distance(direction, h, -1)
            pos = (z + far) % 8
            rs[it, pos, ka, h, p] = own_row(far, h, p)
            push(
                ("zr", direction, 0, h, p), rs.at[it, pos, ka, h, p],
                zb.at[it, direction, 0, h, p], z_next[direction],
            )

        def column_sums(slot):
            for n in range(2):
                for direction, h in chains:
                    if slot < hops(direction, h) - 1:
                        w = 2 * h + n
                        buf = yb.at[it, direction, slot, w]
                        arrived(("yr", direction, slot, w), buf)
                        yb[it, direction, slot, w] += own_column(distance(direction, h, slot), w)
                        push(
                            ("yr", direction, slot + 1, w), buf,
                            yb.at[it, direction, slot + 1, w], y_next[direction],
                        )

        def row_sums(slot):
            for p in range(2):
                for direction, h in chains:
                    if slot < hops(direction, h) - 1:
                        buf = zb.at[it, direction, slot, h, p]
                        arrived(("zr", direction, slot, h, p), buf)
                        zb[it, direction, slot, h, p] += own_row(distance(direction, h, slot), h, p)
                        push(
                            ("zr", direction, slot + 1, h, p), buf,
                            zb.at[it, direction, slot + 1, h, p], z_next[direction],
                        )

        def gram_scatter(d, carry):
            pltpu.make_async_remote_copy(
                src_ref=gm.at[it, (r + d) % 16], dst_ref=gr.at[it, d - 1],
                send_sem=gram_send.at[0], recv_sem=gram_recv.at[it, 0],
                device_id=((r + d) % 16, c), device_id_type=MESH,
            ).start()
            return carry

        def gram_gather(d, carry):
            pltpu.make_async_remote_copy(
                src_ref=gf.at[it, r], dst_ref=gf.at[it, r],
                send_sem=gram_send.at[1], recv_sem=gram_recv.at[it, 1],
                device_id=((r + d) % 16, c), device_id_type=MESH,
            ).start()
            return carry

        def bytes_of_fifteen(sem):
            pltpu.make_async_copy(gr.at[it], gr.at[it], sem).wait()

        def last_sums(box, name, h, *rest):
            total = None
            for direction in range(2):
                slot = hops(direction, h) - 1
                place = (it, direction, slot) + rest
                arrived((name, direction, slot) + rest, box.at[place])
                part = box[place]
                total = part if total is None else total + part
            return total

        row_chunks((4,))
        row_chunks((3, 5))
        column_sums(0)
        for p in range(2):
            for direction, h in chains:
                first_sums(direction, h, p)
        total = jnp.zeros((128, 128), F32)
        for slot in range(4):
            panel = rp[it, :, :, :, slot // 2, slot % 2].reshape(1024, 128)
            total = total + jnp.dot(panel.T, panel, preferred_element_type=F32)
        gm[it] = total.reshape(16, 8, 128)
        lax.fori_loop(1, 16, gram_scatter, 0)
        row_chunks((2, 6))
        column_sums(1)
        row_sums(0)
        row_chunks((1, 7))
        column_sums(2)
        row_sums(1)
        row_chunks((0,))
        bytes_of_fifteen(gram_recv.at[it, 0])
        gf[it, r] = gm[it, r] + jnp.sum(gr[it], axis=0)
        lax.fori_loop(1, 16, gram_gather, 0)
        for w in (0, 2, 1, 3):
            yo[it, w] = own_column(0, w) + last_sums(yb, "yr", w // 2, w)
            n = number(("owner", w))
            copy = pltpu.make_async_remote_copy(
                src_ref=yo.at[it, w], dst_ref=fa.at[it, xh, column_k],
                send_sem=send_sem.at[n], recv_sem=recv_sem.at[it, N_KEYS - 8 + column_k * 2 + xh],
                device_id=stations[w], device_id_type=MESH,
            )
            copy.start()
            sends.append(copy)
        row_sums(2)
        for p in range(2):
            for h in range(2):
                xs[it, h, p] = own_row(0, h, p) + last_sums(zb, "zr", h, h, p)
        push(("xr",), xs.at[it, 1 - xi], xr.at[it], x_peer)
        for k in range(2):
            for h in range(2):
                pltpu.make_async_remote_copy(
                    src_ref=fa.at[it, h, k], dst_ref=fa.at[it, h, k],
                    send_sem=send_sem.at[0], recv_sem=recv_sem.at[it, N_KEYS - 8 + k * 2 + h],
                    device_id=core_peer, device_id_type=MESH,
                ).wait_recv()
            fm[it, k] = fa[it, 0, k] + fa[it, 1, k]
            push(("home", k), fm.at[it, k], fr.at[it, k], served)
        for copy in sends[:-2]:
            copy.wait_send()
        for phase in range(2):
            bytes_of_fifteen(gram_send.at[phase])

        bytes_of_fifteen(gram_recv.at[it, 1])
        held = o_ref[...]
        below = jnp.dot(
            held.reshape(128, 128), gf[it].reshape(128, 128),
            precision=lax.Precision.HIGHEST, preferred_element_type=F32,
        ).reshape(2, 2, 32, 128)
        arrived(("xr",), xr.at[it])
        for k in range(2):
            arrived(("home", k), fr.at[it, k])
        product = xs[it, xi] + xr[it]
        for k in range(2):
            above = product[:, k] + fr[it, k]
            o_ref[:, k] = held[:, k] * (0.5 + 0.5 * above / below[:, k])

        for copy in sends[-2:]:
            copy.wait_send()
        assert len(keys) <= N_KEYS - 8
        return carry

    lax.fori_loop(0, ITERS, sweep, 0)


def shards(tiles, tile_blocks, tile_count, factor):
    vmem = pl.BlockSpec(memory_space=pltpu.VMEM)
    smem = pl.BlockSpec(memory_space=pltpu.SMEM)
    held = pl.pallas_call(
        kernel,
        out_shape=jax.ShapeDtypeStruct((2, 2, 32, 128), F32),
        in_specs=[smem, smem, pl.BlockSpec(memory_space=pl.ANY), vmem],
        out_specs=vmem,
        scratch_shapes=[
            pltpu.VMEM((2, 1024, 1024), BF16),
            pltpu.VMEM((2, 8, 2, 2, 2, 2, 32, 128), BF16),
            pltpu.VMEM((2, 8, 4, 2, 32, 128), BF16),
            pltpu.VMEM((2, 8, 2, 2, 2, 2, 32, 128), F32),
            pltpu.VMEM((2, 8, 2, 2, 2, 32, 128), F32),
            pltpu.VMEM((2, 2, 4, 2, 2, 2, 32, 128), F32),
            pltpu.VMEM((2, 8, 4, 2, 32, 128), F32),
            pltpu.VMEM((2, 2, 4, 4, 2, 32, 128), F32),
            pltpu.VMEM((2, 2, 2, 2, 32, 128), F32),
            pltpu.VMEM((2, 2, 2, 32, 128), F32),
            pltpu.VMEM((2, 2, 2, 32, 128), F32),
            pltpu.VMEM((2, 16, 8, 128), F32),
            pltpu.VMEM((2, 15, 8, 128), F32),
            pltpu.VMEM((2, 16, 8, 128), F32),
            pltpu.VMEM((2, 128, 1024), F32),
            pltpu.VMEM((2, 1024, 128), BF16),
            pltpu.VMEM((2, 4, 2, 32, 128), F32),
            pltpu.VMEM((2, 2, 2, 2, 32, 128), F32),
            pltpu.VMEM((2, 2, 2, 32, 128), F32),
            pltpu.SemaphoreType.DMA,
            pltpu.SemaphoreType.DMA((N_KEYS,)),
            pltpu.SemaphoreType.DMA((2, N_KEYS)),
            pltpu.SemaphoreType.DMA((2,)),
            pltpu.SemaphoreType.DMA((2, 2)),
        ],
        compiler_params=pltpu.CompilerParams(
            collective_id=0, has_side_effects=True, vmem_limit_bytes=50 * 1024 * 1024
        ),
    )(tile_blocks, tile_count, tiles, factor.reshape(2, 2, 32, 128))
    return held.reshape(factor.shape)


def solution(mesh):
    in_specs = (
        P(("row", "col"), None, None),
        P(("row", "col"), None),
        P(("row", "col")),
        P(None, None, "row", "col", None, None),
    )
    out_specs = P(None, None, "row", "col", None, None)
    return jax.shard_map(shards, mesh=mesh, in_specs=in_specs, out_specs=out_specs, check_vma=False)
```

```python
import jax
import jax.numpy as jnp
from jax import lax
from jax.experimental import pallas as pl
from jax.experimental.pallas import tpu as pltpu
from jax.sharding import PartitionSpec as P

ITERS = 2
MESH = pl.DeviceIdType.MESH
F32 = jnp.float32
BF16 = jnp.bfloat16
N_KEYS = 112


def hops(direction, h):
    return 4 if direction == h else 3


def kernel(
    blocks, count, tiles_hbm, f_ref, o_ref,
    tiles, rp, cp, rs, cr, zb, cs, yb, xs, xr, fr, gm, gr, gf, terms, right, yo, fa, fm,
    tile_sem, send_sem, recv_sem, gram_send, gram_recv,
):
    r = lax.axis_index("row")
    c = lax.axis_index("col")
    xh, y = r // 8, r % 8
    z, q = c // 4, c % 4
    xi, ka = q // 2, q % 2

    def spread(t):
        b3, b2, b1, b0 = t // 8, (t // 4) % 2, (t // 2) % 2, t % 2
        return ((2 * b1 + 2 * b3 + 1 - b2 + b0 + 2 * b2 * b0) % 4 + 4 * b2) % 8

    holder_y = (z + 2 * q + spread(r)) % 8
    holders = [[(h * 8 + holder_y, r + 16 * k) for h in range(2)] for k in range(2)]
    owner_row = c % 16
    column_k = c // 16
    shift = spread(owner_row)
    owner_z = [(y + 16 - 2 * w - shift) % 8 for w in range(4)]
    owners = [(owner_row, owner_z[w] * 4 + w) for w in range(4)]

    stations = [
        ((owner_row // 8) * 8 + y, owner_z[w] * 4 + (1 - xi) * 2 + 1 - w % 2) for w in range(4)
    ]
    my_station = (xh * 8 + holder_y, z * 4 + (1 - (r // 2) % 2) * 2 + 1 - ka)
    base = (y + 24 - z - 2 * (1 - ka) - 2 * (1 - xi) - 2 * xh) % 4
    served_row = 8 * xh + 4 * (1 - ((base + 1) % 4) // 2) + 2 * (1 - xi) + base // 2
    served = (served_row, z * 4 + ((y + 16 - z - spread(served_row)) % 8) // 2)
    feeders = [(h * 8 + y, served_row + 16 * k) for k in range(2) for h in range(2)]

    core_peer = (r, z * 4 + xi * 2 + (1 - ka))
    x_peer = (r, z * 4 + (1 - xi) * 2 + ka)
    z_next = [(r, ((z + 1) % 8) * 4 + q), (r, ((z + 7) % 8) * 4 + q)]
    y_next = [(xh * 8 + (y + 1) % 8, c), (xh * 8 + (y + 7) % 8, c)]

    tile_copy = pltpu.make_async_copy(tiles_hbm, tiles, tile_sem)
    tile_copy.start()

    barrier = pltpu.get_barrier_semaphore()
    near = [core_peer, x_peer] + z_next + owners + feeders + [my_station]
    for device in near:
        pl.semaphore_signal(barrier, inc=1, device_id=device, device_id_type=MESH)

    def greet(d, carry):
        pl.semaphore_signal(barrier, inc=1, device_id=((r + d) % 16, c), device_id_type=MESH)
        return carry

    lax.fori_loop(1, 16, greet, 0)
    o_ref[...] = f_ref[...]
    pl.semaphore_wait(barrier, len(near) + 15)

    def source_of(pos, direction, step):
        return (pos + 8 - step) % 8 if direction == 0 else (pos + step) % 8

    def sweep(it, carry):
        keys = {}
        sends = []

        def number(key):
            return keys.setdefault(key, len(keys))

        def push(key, src, dst, device):
            n = number(key)
            copy = pltpu.make_async_remote_copy(
                src_ref=src, dst_ref=dst, send_sem=send_sem.at[n], recv_sem=recv_sem.at[it, n],
                device_id=device, device_id_type=MESH,
            )
            copy.start()
            sends.append(copy)

        def arrived(key, dst):
            n = number(key)
            pltpu.make_async_remote_copy(
                src_ref=dst, dst_ref=dst, send_sem=send_sem.at[n], recv_sem=recv_sem.at[it, n],
                device_id=core_peer, device_id_type=MESH,
            ).wait_recv()

        rp[it, z, xi, ka] = o_ref[...].astype(BF16)
        mine = rp.at[it, z, xi, ka]
        for k in range(2):
            for h in range(2):
                n = number(("scatter", k, h))
                copy = pltpu.make_async_remote_copy(
                    src_ref=rp.at[it, z, xi, ka, :, k], dst_ref=cp.at[it, holder_y, q],
                    send_sem=send_sem.at[n], recv_sem=recv_sem.at[it, N_KEYS - 4 + q],
                    device_id=holders[k][h], device_id_type=MESH,
                )
                copy.start()
                sends.append(copy)

        def chain(h):
            return xi if h == 0 else 1 - xi

        def row_piece(pos, h):
            return rp.at[it, pos, chain(h), ka]

        def column_piece(pos, h):
            return cp.at[it, pos, 2 * h:2 * h + 2]

        def pass_row(direction, step, h):
            pos = source_of(z, direction, step)
            piece = row_piece(pos, h)
            if step > 0:
                arrived(("zg", direction, step, h), piece)
            if step < hops(direction, h):
                push(("zg", direction, step + 1, h), piece, piece, z_next[direction])

        def pass_column(direction, step, h):
            piece = column_piece(source_of(y, direction, step), h)
            if step > 0:
                arrived(("yg", direction, step, h), piece)
            if step < hops(direction, h):
                push(("yg", direction, step + 1, h), piece, piece, y_next[direction])

        def directions(step):
            return (0, 1) if 0 < step < 4 else (0,)

        def across(step):
            for direction in directions(step):
                pieces = rp.at[it, source_of(z, direction, step), :, ka]
                push(("cg", direction, step), pieces, pieces, core_peer)

        def each(passing, step):
            for h in range(2):
                for direction in range(2):
                    if step <= hops(direction, h):
                        passing(direction, step, h)

        live = [(count[0] > s).astype(F32) for s in range(2)]
        off = [(blocks[s, 0] != blocks[s, 1]).astype(F32) for s in range(2)]
        row_slot = [blocks[s, 0] // 16 for s in range(2)]
        is_row = [[(row_slot[s] == slot).astype(F32) for slot in range(4)] for s in range(2)]
        column_slot = [blocks[s, 1] // 32 for s in range(2)]

        def tile_rows(s, pos, columns):
            return tiles[s, pl.ds(pl.multiple_of(pos * 128, 128), 128), columns]

        def joined(parts):
            return parts[0] if len(parts) == 1 else jnp.concatenate(parts, axis=0)

        def chosen(s, pos):
            total = None
            for slot in range(4):
                part = is_row[s][slot] * rp[it, pos, :, :, slot // 2, slot % 2].astype(F32)
                total = part if total is None else total + part
            return total.reshape(128, 128).astype(BF16)

        def panel_step(step):
            for direction in directions(step):
                arrived(("cg", direction, step), rp.at[it, source_of(z, direction, step), :, 1 - ka])
            places = [source_of(z, direction, step) for direction in directions(step)]
            for s in range(2):
                left = joined([chosen(s, pos) for pos in places]).T
                for n in range(4):
                    columns = slice(n * 256, (n + 1) * 256)
                    term = jnp.dot(
                        left, joined([tile_rows(s, pos, columns) for pos in places]),
                        preferred_element_type=F32,
                    )
                    if step == 0:
                        terms[s, :, columns] = term
                    else:
                        terms[s, :, columns] += term
            total = None
            for pos in places:
                panel = rp[it, pos].reshape(512, 128)
                part = jnp.dot(panel.T, panel, preferred_element_type=F32).reshape(16, 8, 128)
                total = part if total is None else total + part
            if step == 0:
                gm[it] = total
            else:
                gm[it] += total

        push(("x",), mine, mine, x_peer)
        for direction in range(2):
            pass_row(direction, 0, 0)
        arrived(("x",), row_piece(z, 1))
        for direction in range(2):
            pass_row(direction, 0, 1)
        across(0)
        each(pass_row, 1)
        across(1)
        for h in range(2):
            for w in (2 * h, 2 * h + 1):
                pltpu.make_async_remote_copy(
                    src_ref=cp.at[it, y, w], dst_ref=cp.at[it, y, w],
                    send_sem=send_sem.at[0], recv_sem=recv_sem.at[it, N_KEYS - 4 + w],
                    device_id=core_peer, device_id_type=MESH,
                ).wait_recv()
            for direction in range(2):
                pass_column(direction, 0, h)
        each(pass_row, 2)
        across(2)
        each(pass_column, 1)

        @pl.when(it == 0)
        def _():
            tile_copy.wait()

        panel_step(0)
        each(pass_row, 3)
        across(3)
        each(pass_column, 2)
        panel_step(1)
        each(pass_row, 4)
        across(4)
        each(pass_column, 3)
        panel_step(2)
        panel_step(3)
        panel_step(4)
        for p in range(2):
            weight = [live[s] * off[s] * (column_slot[s] == p).astype(F32) for s in range(2)]
            for n in range(8):
                columns = slice(n * 128, (n + 1) * 128)
                both = (weight[0] * terms[0, :, columns] + weight[1] * terms[1, :, columns]).T
                for w in range(4):
                    cs[it, (n + 2 * w + shift) % 8, w, p] = both[w * 32:w * 32 + 32]

        def distance(direction, h, slot):
            ahead = hops(direction, h) - 1 - slot
            return ahead if direction == 0 else (8 - ahead) % 8

        chains = ((0, 0), (1, 1), (0, 1), (1, 0))
        for direction, h in chains:
            push(
                ("yr", direction, 0, h), cs.at[it, (y + distance(direction, h, -1)) % 8, 2 * h:2 * h + 2],
                yb.at[it, direction, 0, h], y_next[direction],
            )
        each(pass_column, 4)

        for s in range(2):
            for v in range(32):
                right[s, v * 32:v * 32 + 32, :] = cp[
                    it, (v // 4 + 2 * (v % 4) + shift) % 8, v % 4, column_slot[s]
                ]

        def row_chunks(fars):
            places = [(z + far) % 8 for far in fars]
            term = [
                jnp.dot(
                    joined([tile_rows(s, pos, slice(None)) for pos in places]), right[s],
                    preferred_element_type=F32,
                )
                for s in range(2)
            ]
            for slot in range(4):
                weight = [live[s] * (row_slot[s] == slot).astype(F32) for s in range(2)]
                both = weight[0] * term[0] + weight[1] * term[1]
                for n, pos in enumerate(places):
                    for w in range(4):
                        rows = slice(n * 128 + w * 32, n * 128 + w * 32 + 32)
                        rs[it, pos, w % 2, w // 2, slot // 2, slot % 2] = both[rows]
            for far, pos in zip(fars, places):
                push(("cr", far), rs.at[it, pos, 1 - ka], cr.at[it, pos], core_peer)

        met = set()

        def own_row(far, h):
            pos = (z + far) % 8
            if far not in met:
                met.add(far)
                arrived(("cr", far), cr.at[it, pos])
            return rs[it, pos, ka, h] + cr[it, pos, h]

        def own_column(far, h):
            return cs[it, (y + far) % 8, 2 * h:2 * h + 2]

        def first_sums(direction, h):
            far = distance(direction, h, -1)
            pos = (z + far) % 8
            rs[it, pos, ka, h] = own_row(far, h)
            push(
                ("zr", direction, 0, h), rs.at[it, pos, ka, h],
                zb.at[it, direction, 0, h], z_next[direction],
            )

        def column_sums(slot):
            for direction, h in chains:
                if slot < hops(direction, h) - 1:
                    buf = yb.at[it, direction, slot, h]
                    arrived(("yr", direction, slot, h), buf)
                    yb[it, direction, slot, h] += own_column(distance(direction, h, slot), h)
                    push(("yr", direction, slot + 1, h), buf, yb.at[it, direction, slot + 1, h], y_next[direction])

        def row_sums(slot):
            for direction, h in chains:
                if slot < hops(direction, h) - 1:
                    buf = zb.at[it, direction, slot, h]
                    arrived(("zr", direction, slot, h), buf)
                    zb[it, direction, slot, h] += own_row(distance(direction, h, slot), h)
                    push(("zr", direction, slot + 1, h), buf, zb.at[it, direction, slot + 1, h], z_next[direction])

        mine_to_sum = r % 4 == q

        def gram_scatter(m, carry):
            target = 4 * m + q

            @pl.when(target != r)
            def _():
                pltpu.make_async_remote_copy(
                    src_ref=gm.at[it, target], dst_ref=gr.at[it, (target + 16 - r) % 16 - 1],
                    send_sem=gram_send.at[0], recv_sem=gram_recv.at[it, 0],
                    device_id=(target, c), device_id_type=MESH,
                ).start()

            return carry

        def gram_gather(d, carry):
            piece = gf.at[it, r // 4, xi, ka]
            pltpu.make_async_remote_copy(
                src_ref=piece, dst_ref=piece,
                send_sem=gram_send.at[1], recv_sem=gram_recv.at[it, 1],
                device_id=((r + d) % 16, c), device_id_type=MESH,
            ).start()
            return carry

        def bytes_of(pieces, sem):
            box = gr.at[it, 0:pieces]
            pltpu.make_async_copy(box, box, sem).wait()

        def bytes_of_group(sem):
            @pl.when(mine_to_sum)
            def _():
                bytes_of(3, sem)

            @pl.when(jnp.logical_not(mine_to_sum))
            def _():
                bytes_of(4, sem)

        def last_sums(box, name, h):
            total = None
            for direction in range(2):
                slot = hops(direction, h) - 1
                arrived((name, direction, slot, h), box.at[it, direction, slot, h])
                part = box[it, direction, slot, h]
                total = part if total is None else total + part
            return total

        row_chunks((4,))
        row_chunks((3, 5))
        column_sums(0)
        for direction, h in chains:
            first_sums(direction, h)
        lax.fori_loop(0, 4, gram_scatter, 0)
        row_chunks((2, 6))
        column_sums(1)
        row_sums(0)
        row_chunks((1, 7))
        column_sums(2)
        row_sums(1)
        row_chunks((0,))

        @pl.when(mine_to_sum)
        def _():
            bytes_of(15, gram_recv.at[it, 0])
            gf[it, r // 4, xi, ka] = gm[it, r] + jnp.sum(gr[it], axis=0)
            lax.fori_loop(1, 16, gram_gather, 0)

        for h in range(2):
            yo[it, h] = own_column(0, h) + last_sums(yb, "yr", h)
            for w in range(2):
                n = number(("owner", 2 * h + w))
                copy = pltpu.make_async_remote_copy(
                    src_ref=yo.at[it, h, w], dst_ref=fa.at[it, xh, column_k],
                    send_sem=send_sem.at[n], recv_sem=recv_sem.at[it, N_KEYS - 8 + column_k * 2 + xh],
                    device_id=stations[2 * h + w], device_id_type=MESH,
                )
                copy.start()
                sends.append(copy)
        row_sums(2)
        bytes_of_group(gram_recv.at[it, 1])
        push(("gc",), gf.at[it, :, xi, ka], gf.at[it, :, xi, ka], core_peer)
        for h in range(2):
            xs[it, h] = own_row(0, h) + last_sums(zb, "zr", h)
        push(("xr",), xs.at[it, 1 - xi], xr.at[it], x_peer)
        arrived(("gc",), gf.at[it, :, xi, 1 - ka])
        push(("gx",), gf.at[it, :, xi], gf.at[it, :, xi], x_peer)
        for k in range(2):
            for h in range(2):
                pltpu.make_async_remote_copy(
                    src_ref=fa.at[it, h, k], dst_ref=fa.at[it, h, k],
                    send_sem=send_sem.at[0], recv_sem=recv_sem.at[it, N_KEYS - 8 + k * 2 + h],
                    device_id=core_peer, device_id_type=MESH,
                ).wait_recv()
        fm[it] = fa[it, 0] + fa[it, 1]
        push(("home",), fm.at[it], fr.at[it], served)

        arrived(("gx",), gf.at[it, :, 1 - xi])
        held = o_ref[...]
        below = jnp.dot(
            held.reshape(128, 128), gf[it].reshape(128, 128),
            precision=lax.Precision.HIGHEST, preferred_element_type=F32,
        ).reshape(2, 2, 32, 128)
        arrived(("xr",), xr.at[it])
        arrived(("home",), fr.at[it])
        product = xs[it, xi] + xr[it]
        for k in range(2):
            above = product[:, k] + fr[it, k]
            o_ref[:, k] = held[:, k] * (0.5 + 0.5 * above / below[:, k])

        for copy in sends:
            copy.wait_send()
        bytes_of_group(gram_send.at[0])

        @pl.when(mine_to_sum)
        def _():
            bytes_of(15, gram_send.at[1])

        assert len(keys) <= N_KEYS - 8
        return carry

    lax.fori_loop(0, ITERS, sweep, 0)


def shards(tiles, tile_blocks, tile_count, factor):
    vmem = pl.BlockSpec(memory_space=pltpu.VMEM)
    smem = pl.BlockSpec(memory_space=pltpu.SMEM)
    held = pl.pallas_call(
        kernel,
        out_shape=jax.ShapeDtypeStruct((2, 2, 32, 128), F32),
        in_specs=[smem, smem, pl.BlockSpec(memory_space=pl.ANY), vmem],
        out_specs=vmem,
        scratch_shapes=[
            pltpu.VMEM((2, 1024, 1024), BF16),
            pltpu.VMEM((2, 8, 2, 2, 2, 2, 32, 128), BF16),
            pltpu.VMEM((2, 8, 4, 2, 32, 128), BF16),
            pltpu.VMEM((2, 8, 2, 2, 2, 2, 32, 128), F32),
            pltpu.VMEM((2, 8, 2, 2, 2, 32, 128), F32),
            pltpu.VMEM((2, 2, 4, 2, 2, 2, 32, 128), F32),
            pltpu.VMEM((2, 8, 4, 2, 32, 128), F32),
            pltpu.VMEM((2, 2, 4, 2, 2, 2, 32, 128), F32),
            pltpu.VMEM((2, 2, 2, 2, 32, 128), F32),
            pltpu.VMEM((2, 2, 2, 32, 128), F32),
            pltpu.VMEM((2, 2, 2, 32, 128), F32),
            pltpu.VMEM((2, 16, 8, 128), F32),
            pltpu.VMEM((2, 15, 8, 128), F32),
            pltpu.VMEM((2, 4, 2, 2, 8, 128), F32),
            pltpu.VMEM((2, 128, 1024), F32),
            pltpu.VMEM((2, 1024, 128), BF16),
            pltpu.VMEM((2, 2, 2, 2, 32, 128), F32),
            pltpu.VMEM((2, 2, 2, 2, 32, 128), F32),
            pltpu.VMEM((2, 2, 2, 32, 128), F32),
            pltpu.SemaphoreType.DMA,
            pltpu.SemaphoreType.DMA((N_KEYS,)),
            pltpu.SemaphoreType.DMA((2, N_KEYS)),
            pltpu.SemaphoreType.DMA((2,)),
            pltpu.SemaphoreType.DMA((2, 2)),
        ],
        compiler_params=pltpu.CompilerParams(
            collective_id=0, has_side_effects=True, vmem_limit_bytes=50 * 1024 * 1024
        ),
    )(tile_blocks, tile_count, tiles, factor.reshape(2, 2, 32, 128))
    return held.reshape(factor.shape)


def solution(mesh):
    in_specs = (
        P(("row", "col"), None, None),
        P(("row", "col"), None),
        P(("row", "col")),
        P(None, None, "row", "col", None, None),
    )
    out_specs = P(None, None, "row", "col", None, None)
    return jax.shard_map(shards, mesh=mesh, in_specs=in_specs, out_specs=out_specs, check_vma=False)
```
